128 devices in a mesh: gx: 8 (over x, z_hi), gy: 16 (over y, z_lo, core).
Axes of the slice: x: 4, y: 4, z: 4 (z_hi: 2, z_lo: 2; z = z_hi * 2 + z_lo), core: 2. Of those that a mesh axis runs over, the one named last changes fastest.
Arguments:
- weights: float32 [1048576, 128], P(('gx', 'gy')), may hold values from -0.625 to 0.625
- phases: float32 [7, 524288, 128], P(None, ('gx', 'gy')), may hold values from -3.140625 to 3.140625
Outputs:
- result: float32 [1048576, 128], P(('gx', 'gy'))
The draws below stay inside these ranges and needn't reach their ends.
All inputs are finite; a program needn't handle non-finite values.
Results may differ from the reference program's by a relative error of at most 0.00012.
Values sent between devices are 32-bit elements; how exact they have to be, the bound alone decides.
A program may use at most 192 MiB of HBM per device.

```python
import math
import jax
import jax.numpy as jnp
from jax import lax

RANK = 64
TARGETS = 8192
LEVELS = 7
BOXES = 128
N_GX = 8
N_GY = 16


def levels(key, extent, split, least, top_value):
    def one(dim, parts):
        heights = jax.random.uniform(jax.random.fold_in(jax.random.fold_in(key, 6), dim), (parts,), jnp.float32, least / len(split), top_value / len(split))
        return jnp.repeat(jnp.exp(heights), extent[dim] // parts).reshape((-1,) + (1,) * (len(extent) - dim - 1))

    gain = one(*split[0])
    for cut in split[1:]:
        gain = gain * one(*cut)
    return gain


def normal_values(own_key, shape, width, limit, pieces=(), kind=jnp.bfloat16):
    array = width * jax.random.normal(own_key, shape, jnp.float32)
    if pieces:
        array = array * levels(own_key, shape, pieces, -0.22, 0.18)
    return jnp.clip(array, -limit, limit).astype(kind)


def setup_inputs(seed: int = 0) -> dict:
    arg_keys = jax.random.split(jax.random.key(seed), 3)
    return {
        "weights": normal_values(arg_keys[0], (BOXES * TARGETS, 2 * RANK), 0.1, 0.625, ((0, 128),), jnp.float32),
        "phases": jnp.clip(jax.random.uniform(arg_keys[1], (LEVELS, BOXES * TARGETS // 2, 2 * RANK), jnp.float32, -3.140625, 3.140625), -3.140625, 3.140625),
    }


def level_matrices():
    node_index = jnp.arange(8, dtype=jnp.float32)
    cheb_nodes = jnp.cos((2.0 * node_index + 1.0) * math.pi / 16.0)
    eye_side = jnp.eye(8, dtype=jnp.float32)
    eye_pair = jnp.eye(2, dtype=jnp.float32)
    diagonal_mask = jnp.arange(8)[:, None, None] == jnp.arange(8)[None, None, :]
    along_one = []
    along_two = []
    for child_index in range(2):
        points = (cheb_nodes + (2.0 * child_index - 1.0)) * 0.5
        numerators = points[None, :, None] - cheb_nodes[None, None, :]
        denominators = cheb_nodes[:, None, None] - cheb_nodes[None, None, :]
        factor = jnp.where(diagonal_mask, 1.0, numerators / jnp.where(diagonal_mask, 1.0, denominators))
        lagrange = jnp.prod(factor, axis=2)
        along_one.append(jnp.kron(eye_pair, jnp.kron(lagrange, eye_side)))
        along_two.append(jnp.kron(eye_pair, jnp.kron(eye_side, lagrange)))
    return jnp.concatenate(along_one, axis=1), jnp.concatenate(along_two, axis=1)


def modulate(values, angle_rows):
    rank_size = angle_rows.shape[-1]
    real_part = values[..., :rank_size]
    imag_part = values[..., rank_size:]
    cosine = jnp.cos(angle_rows)
    sine_part = jnp.sin(angle_rows)
    return jnp.concatenate([cosine * real_part - sine_part * imag_part, sine_part * real_part + cosine * imag_part], axis=-1)


def reference(weights, phases):
    box_count = N_GX * N_GY
    half_rows = TARGETS // 2
    angles = phases.reshape(LEVELS, box_count, TARGETS, RANK)
    matrices = level_matrices()
    gx_bits = int(N_GX).bit_length() - 1
    gy_bits = int(N_GY).bit_length() - 1
    plan = [(gy_bits + bit_pos, 0) for bit_pos in reversed(range(gx_bits))]
    plan = plan + [(bit_pos, 1) for bit_pos in reversed(range(gy_bits))]
    current = weights.reshape(box_count, TARGETS, 2 * RANK)
    for level_index, (position, dim_index) in enumerate(plan):
        modulated = modulate(current, angles[level_index])
        outer_count = box_count // (2 ** (position + 1))
        inner_count = 2 ** position
        modulated = modulated.reshape(outer_count, 2, inner_count, 2, half_rows, 2 * RANK)
        combined = modulated[:, 0] + modulated[:, 1]
        combined = jnp.moveaxis(combined, 2, 1)
        refined = jnp.dot(combined.reshape(-1, 2 * RANK), matrices[dim_index], precision=lax.Precision.HIGHEST, preferred_element_type=jnp.float32)
        current = refined.reshape(box_count, TARGETS, 2 * RANK)
    return current.reshape(box_count * TARGETS, 2 * RANK)
```

```python
import functools
import math

import jax
import jax.numpy as jnp
import numpy as np
from jax import lax
from jax.experimental import pallas as pl
from jax.experimental.pallas import tpu as pltpu
from jax.sharding import PartitionSpec as P

MESH = pl.DeviceIdType.MESH
LEVELS = 7
CHUNK_BITS = 4
CHUNKS = 1 << CHUNK_BITS
ROWS = 4096 // CHUNKS
HALF = ROWS // 2
DEPTH = 2
SLOTS = 4
AHEAD = 3


def low_bits(level):
    return 5 - CHUNK_BITS + level


def unit_rows(level):
    return max(8, 1 << low_bits(level))


def units(level):
    return (1 << (5 + level)) // unit_rows(level)


def sel_count(level):
    return 1 << (7 - level)


def chunks_per_unit(level):
    return CHUNKS // units(level)


def series(func, degree):
    top = 3.140625**2
    nodes = (np.cos((np.arange(64) + 0.5) * np.pi / 64) + 1.0) * top / 2
    fit = np.polynomial.chebyshev.Chebyshev.fit(nodes, func(np.sqrt(nodes)), degree, domain=[0.0, top])
    return [float(np.float32(c)) for c in fit.convert(kind=np.polynomial.Polynomial).coef]


COS_COEF = series(np.cos, 6)
SIN_COEF = series(lambda r: np.sin(r) / r, 5)


def horner(coef, square):
    total = jnp.full_like(square, coef[-1])
    total = coef[-1] * square + coef[-2]
    for c in reversed(coef[:-2]):
        total = total * square + c
    return total


def cos_sin(angle):
    square = angle * angle
    return horner(COS_COEF, square), horner(SIN_COEF, square) * angle


def refine_matrices():
    nodes = np.cos((2.0 * np.arange(8) + 1.0) * math.pi / 16.0)
    sides = []
    for child in range(2):
        points = (nodes + 2.0 * child - 1.0) / 2.0
        lagrange = np.ones((8, 8))
        for j in range(8):
            for m in range(8):
                if m != j:
                    lagrange[j] *= (points - nodes[m]) / (nodes[j] - nodes[m])
        sides.append(lagrange)
    eye = np.eye(8)
    first = np.concatenate([np.kron(k, eye) for k in sides], axis=1)
    second = np.concatenate([np.kron(eye, k) for k in sides], axis=1)
    zero = np.zeros_like(first)

    def split(matrix):
        matrix = np.asarray(matrix, np.float32)
        high = matrix.astype(jnp.bfloat16)
        low = (matrix - high.astype(np.float32)).astype(jnp.bfloat16)
        return high, low

    mats = []
    for pair in (first, second):
        high, low = split(np.block([[pair, zero], [zero, pair]]))
        mats.append(np.stack([np.concatenate([high, high]), np.concatenate([low, low])]))
    last = np.zeros((256, 512))
    for slot in range(2):
        for child in range(2):
            edge = second[:, 64 * child : 64 * child + 64]
            col = 256 * slot + 128 * child
            last[64 * slot : 64 * slot + 64, col : col + 64] = edge
            last[128 + 64 * slot : 192 + 64 * slot, col + 64 : col + 128] = edge
    high, low = split(last)
    return np.stack(mats), np.stack([high, low])


def split_value(x):
    high = x.astype(jnp.bfloat16)
    low = (x - high.astype(jnp.float32)).astype(jnp.bfloat16)
    return high, low


def dot(a, b):
    return jnp.dot(a, b, preferred_element_type=jnp.float32)


def kernel(w_ref, *refs):
    p_refs = refs[:LEVELS]
    mats_ref, last_ref, out_ref = refs[LEVELS : LEVELS + 3]
    w_buf = refs[LEVELS + 3]
    p_bufs = refs[LEVELS + 4 : 2 * LEVELS + 4]
    mod, recv, staged, w_sem, p_sem, send_sem, recv_sem, out_sem = refs[2 * LEVELS + 4 :]

    gx = lax.axis_index("gx")
    gy = lax.axis_index("gy")
    own = []
    partner = []
    for level in range(LEVELS):
        if level < 3:
            weight = 1 << (2 - level)
            bit = (gx // weight) % 2
            partner.append((gx + weight - 2 * weight * bit, gy))
        else:
            weight = 1 << (6 - level)
            bit = (gy // weight) % 2
            partner.append((gx, gy + weight - 2 * weight * bit))
        own.append(bit)

    barrier = pltpu.get_barrier_semaphore()
    for device in partner:
        pl.semaphore_signal(barrier, inc=1, device_id=device, device_id_type=MESH)

    def weight_copy(unit):
        return pltpu.make_async_copy(w_ref.at[:, unit], w_buf.at[unit], w_sem.at[unit])

    def phase_copy(level, unit):
        return pltpu.make_async_copy(
            p_refs[level].at[level, :, unit], p_bufs[level].at[unit], p_sem.at[level, unit]
        )

    def exchange(level, chunk):
        slot = chunk % SLOTS
        return pltpu.make_async_remote_copy(
            src_ref=mod.at[level, slot, 1 - own[level]],
            dst_ref=recv.at[level, chunk],
            send_sem=send_sem.at[level, slot],
            recv_sem=recv_sem.at[level, chunk],
            device_id=partner[level],
            device_id_type=MESH,
        )

    def out_copy(chunk):
        return pltpu.make_async_copy(
            staged.at[chunk], out_ref.at[pl.ds(chunk * 2 * ROWS, 2 * ROWS)], out_sem.at[chunk]
        )

    def phase_rows(level, chunk, offset, count, stride):
        per = chunks_per_unit(level)
        flat = p_bufs[level].at[chunk // per].reshape(sel_count(level) * unit_rows(level), 128)
        start = (chunk % per) * (1 << low_bits(level)) + offset if per > 1 else offset
        return flat[pl.ds(start, count, stride=stride)]

    def put(level, slot, half, start, real, imag, angle):
        cosine, sine = cos_sin(angle)
        rows = pl.ds(start, real.shape[0])
        mod[level, slot, half, 0, rows] = cosine * real - sine * imag
        mod[level, slot, half, 1, rows] = sine * real + cosine * imag

    def first_stage(chunk):
        per = chunks_per_unit(0)
        unit = chunk // per
        slot = chunk % SLOTS
        flat = w_buf.at[unit].reshape(128 * 16, 128)
        left = lax.broadcasted_iota(jnp.int32, (64, 128), 1) < 64
        for u in range(1 << low_bits(0)):
            row = (chunk % per) * (1 << low_bits(0)) + u
            for half in range(2):
                even = flat[pl.ds(half * 64 * 16 + 2 * row, 64, stride=16)]
                odd = flat[pl.ds(half * 64 * 16 + 2 * row + 1, 64, stride=16)]
                real = jnp.where(left, even, pltpu.roll(odd, 64, 1))
                imag = jnp.where(left, pltpu.roll(even, 64, 1), odd)
                angle = phase_rows(0, chunk, half * 64 * 8 + u, 64, 8)
                put(0, slot, half, u * 64, real, imag, angle)

    def joined(level, chunk):
        slot = chunk % SLOTS
        both = []
        for part in range(2):
            if level == 3:
                step = HALF // 8
                pieces = []
                for s in range(8):
                    rows = pl.ds(s, step, stride=8)
                    pieces.append(
                        mod.at[level, slot, own[level], part][rows] + recv.at[level, chunk, part][rows]
                    )
                both.append(jnp.concatenate(pieces, axis=0))
            else:
                both.append(mod[level, slot, own[level], part] + recv[level, chunk, part])
        return both

    def interpolate(level, chunk):
        real, imag = joined(level, chunk)
        high, low = split_value(jnp.concatenate([real, imag], axis=0))
        wide = jnp.concatenate([high, low], axis=1)
        which = 0 if level < 3 else 1
        out = dot(wide, mats_ref[which, 0]) + dot(wide, mats_ref[which, 1])
        return out[:HALF], out[HALF:]

    def middle_stage(level, chunk):
        real, imag = interpolate(level - 1, chunk)
        slot = chunk % SLOTS
        if level <= 3:
            sel = sel_count(level)
            part = sel // 2
            stride = unit_rows(level)
            for u in range(HALF // sel):
                for i in range(2):
                    for half in range(2):
                        rows = slice(u * sel + half * part, u * sel + half * part + part)
                        lanes = slice(i * 128, i * 128 + 128)
                        angle = phase_rows(level, chunk, half * part * stride + 2 * u + i, part, stride)
                        put(level, slot, half, (2 * u + i) * part, real[rows, lanes], imag[rows, lanes], angle)
        else:
            lows = 1 << (level - 4)
            size = HALF // lows
            part = size // 2
            for half in range(2):
                for low in range(lows):
                    for i in range(2):
                        rows = slice(low * size + half * part, low * size + half * part + part)
                        lanes = slice(i * 128, i * 128 + 128)
                        angle = phase_rows(level, chunk, half * HALF + 2 * low + i, part, 2 * lows)
                        put(level, slot, half, (2 * low + i) * part, real[rows, lanes], imag[rows, lanes], angle)

    def last_stage(chunk):
        real, imag = joined(LEVELS - 1, chunk)
        high, low = split_value(jnp.concatenate([real, imag], axis=1))
        out = dot(high, last_ref[0]) + dot(low, last_ref[0]) + dot(high, last_ref[1])
        size = HALF // 8
        for low_row in range(8):
            for k in range(4):
                staged.at[chunk][pl.ds(low_row * 4 + k, size, stride=32)] = out[
                    low_row * size : low_row * size + size, k * 128 : k * 128 + 128
                ]

    def step(time, carry):
        for level in range(LEVELS):
            ahead = time + AHEAD - level * DEPTH
            per = chunks_per_unit(level)

            @pl.when((ahead >= 0) & (ahead < CHUNKS) & (ahead % per == 0))
            def _():
                phase_copy(level, ahead // per).start()
                if level == 0:
                    weight_copy(ahead // per).start()

        for stage in range(LEVELS + 1):
            chunk = time - stage * DEPTH

            @pl.when((chunk >= 0) & (chunk < CHUNKS))
            def _():
                if stage > 0:
                    exchange(stage - 1, chunk).wait_recv()
                if stage < LEVELS:
                    per = chunks_per_unit(stage)

                    @pl.when(chunk % per == 0)
                    def _():
                        phase_copy(stage, chunk // per).wait()
                        if stage == 0:
                            weight_copy(chunk // per).wait()

                    @pl.when(chunk >= SLOTS)
                    def _():
                        exchange(stage, chunk - SLOTS).wait_send()

                if stage == 0:
                    first_stage(chunk)
                elif stage < LEVELS:
                    middle_stage(stage, chunk)
                else:
                    last_stage(chunk)
                if stage == 0:

                    @pl.when(chunk == 0)
                    def _():
                        pl.semaphore_wait(barrier, LEVELS)

                if stage < LEVELS:
                    exchange(stage, chunk).start()
                else:
                    out_copy(chunk).start()

        return carry

    lax.fori_loop(-AHEAD, CHUNKS + LEVELS * DEPTH, step, 0)

    def finish(chunk, carry):
        for level in range(LEVELS):
            exchange(level, chunk).wait_send()
        return carry

    lax.fori_loop(CHUNKS - SLOTS, CHUNKS, finish, 0)

    def drain(chunk, carry):
        out_copy(chunk).wait()
        return carry

    lax.fori_loop(0, CHUNKS, drain, 0)


def shards(weights, phases):
    mats, last = refine_matrices()
    views = [
        phases.reshape(LEVELS, sel_count(level), units(level), unit_rows(level), 128)
        for level in range(LEVELS)
    ]
    anywhere = pl.BlockSpec(memory_space=pl.ANY)
    vmem = pl.BlockSpec(memory_space=pltpu.VMEM)
    scratch = [pltpu.VMEM((4, 128, 16, 128), jnp.float32)]
    scratch += [
        pltpu.VMEM((units(level), sel_count(level), unit_rows(level), 128), jnp.float32)
        for level in range(LEVELS)
    ]
    scratch += [
        pltpu.VMEM((LEVELS, SLOTS, 2, 2, HALF, 128), jnp.float32),
        pltpu.VMEM((LEVELS, CHUNKS, 2, HALF, 128), jnp.float32),
        pltpu.VMEM((CHUNKS, 2 * ROWS, 128), jnp.float32),
        pltpu.SemaphoreType.DMA((4,)),
        pltpu.SemaphoreType.DMA((LEVELS, CHUNKS)),
        pltpu.SemaphoreType.DMA((LEVELS, SLOTS)),
        pltpu.SemaphoreType.DMA((LEVELS, CHUNKS)),
        pltpu.SemaphoreType.DMA((CHUNKS,)),
    ]
    return pl.pallas_call(
        kernel,
        out_shape=jax.ShapeDtypeStruct(weights.shape, jnp.float32),
        in_specs=[anywhere] * (LEVELS + 1) + [vmem] * 2,
        out_specs=anywhere,
        scratch_shapes=scratch,
        compiler_params=pltpu.CompilerParams(
            collective_id=0, has_side_effects=True, vmem_limit_bytes=58 * 2**20
        ),
    )(weights.reshape(128, 4, 16, 128), *views, jnp.asarray(mats), jnp.asarray(last))


def solution(mesh):
    return jax.shard_map(
        shards,
        mesh=mesh,
        in_specs=(P(("gx", "gy"), None), P(None, ("gx", "gy"), None)),
        out_specs=P(("gx", "gy"), None),
        check_vma=False,
    )
```

```python
import functools
import math

import jax
import jax.numpy as jnp
import numpy as np
from jax import lax
from jax.experimental import pallas as pl
from jax.experimental.pallas import tpu as pltpu
from jax.sharding import PartitionSpec as P

MESH = pl.DeviceIdType.MESH
LEVELS = 7
CHUNK_BITS = 4
CHUNKS = 1 << CHUNK_BITS
ROWS = 4096 // CHUNKS
HALF = ROWS // 2
LOW = 1 << (7 - CHUNK_BITS)
STAGES = 6
DEPTH = 2
SLOTS = 4
AHEAD = 3
LOCAL_SLOTS = 4
STATIC_SLOTS = 4
BOXES = (1, 2, 2, 4, 2, 2, 2)
PICKED = (128, 32, 16, 4, 4, 2, 1)
STAGE_OF = (0, 1, 2, 3, 3, 4, 5)
SEND_AT = (0, 0, 0, 0, 0, 0, 0)
PARTNERS = (3, 1, 3, 1, 1)


def low_bits(level):
    return 5 - CHUNK_BITS + level


def unit_rows(level):
    return max(8, 1 << low_bits(level))


def units(level):
    return (1 << (5 + level)) // unit_rows(level)


def sel_count(level):
    return 1 << (7 - level)


def chunks_per_unit(level):
    return CHUNKS // units(level)


def series(func, degree):
    top = 3.140625**2
    nodes = (np.cos((np.arange(64) + 0.5) * np.pi / 64) + 1.0) * top / 2
    fit = np.polynomial.chebyshev.Chebyshev.fit(nodes, func(np.sqrt(nodes)), degree, domain=[0.0, top])
    return [float(np.float32(c)) for c in fit.convert(kind=np.polynomial.Polynomial).coef]


COS_COEF = series(np.cos, 6)
SIN_COEF = series(lambda r: np.sin(r) / r, 5)


def horner(coef, square):
    total = jnp.full_like(square, coef[-1])
    total = coef[-1] * square + coef[-2]
    for c in reversed(coef[:-2]):
        total = total * square + c
    return total


def cos_sin(angle):
    square = angle * angle
    return horner(COS_COEF, square), horner(SIN_COEF, square) * angle


def refine_matrices():
    nodes = np.cos((2.0 * np.arange(8) + 1.0) * math.pi / 16.0)
    sides = []
    for child in range(2):
        points = (nodes + 2.0 * child - 1.0) / 2.0
        lagrange = np.ones((8, 8))
        for j in range(8):
            for m in range(8):
                if m != j:
                    lagrange[j] *= (points - nodes[m]) / (nodes[j] - nodes[m])
        sides.append(lagrange)
    eye = np.eye(8)
    first = np.concatenate([np.kron(k, eye) for k in sides], axis=1)
    second = np.concatenate([np.kron(eye, k) for k in sides], axis=1)
    zero = np.zeros_like(first)

    def split(matrix):
        matrix = np.asarray(matrix, np.float32)
        high = matrix.astype(jnp.bfloat16)
        low = (matrix - high.astype(np.float32)).astype(jnp.bfloat16)
        return high, low

    mats = []
    for pair in (first, second):
        high, low = split(np.block([[pair, zero], [zero, pair]]))
        mats.append(np.stack([np.concatenate([high, high]), np.concatenate([low, low])]))
    last = np.zeros((256, 512))
    for slot in range(2):
        for child in range(2):
            edge = second[:, 64 * child : 64 * child + 64]
            col = 256 * slot + 128 * child
            last[64 * slot : 64 * slot + 64, col : col + 64] = edge
            last[128 + 64 * slot : 192 + 64 * slot, col + 64 : col + 128] = edge
    high, low = split(last)
    return np.stack(mats), np.stack([high, low])


def split_value(x):
    high = x.astype(jnp.bfloat16)
    low = (x - high.astype(jnp.float32)).astype(jnp.bfloat16)
    return high, low


def stacked_dot(blocks, mats, which):
    high, low = split_value(jnp.concatenate(blocks, axis=0))
    wide = jnp.concatenate([high, low], axis=1)
    return dot(wide, mats[which, 0]) + dot(wide, mats[which, 1])


def turned(real, imag, angle):
    cosine, sine = cos_sin(angle)
    return cosine * real - sine * imag, sine * real + cosine * imag


def dot(a, b):
    return jnp.dot(a, b, preferred_element_type=jnp.float32)


def kernel(w_ref, *refs):
    p_refs = refs[:LEVELS]
    mats_ref, last_ref, out_ref = refs[LEVELS : LEVELS + 3]
    w_buf = refs[LEVELS + 3]
    p_bufs = refs[LEVELS + 4 : 2 * LEVELS + 4]
    held = refs[2 * LEVELS + 4 : 2 * LEVELS + 9]
    came = refs[2 * LEVELS + 9 : 2 * LEVELS + 14]
    staged, w_sem, p_sem, give_sem, get_sem, send_sem, recv_sem, out_sem = refs[2 * LEVELS + 14 :]

    gx = lax.axis_index("gx")
    gy = lax.axis_index("gy")
    x, z_high = gx // 2, gx % 2
    y, z_low, core = gy // 4, (gy // 2) % 2, gy % 2

    def flips(v):
        return (v, v + 1 - 2 * (v % 2), (v + 2) % 4, 3 - v)

    x_flips = flips(x)
    y_flips = flips(y)
    to_x = [(x_flips[j] * 2 + z_high, gy) for j in range(1, 4)]
    to_z_high = (gx + 1 - 2 * z_high, gy)
    to_y = [(gx, y_flips[j] * 4 + z_low * 2 + core) for j in range(1, 4)]
    to_z_low = (gx, gy + 2 - 4 * z_low)
    to_core = (gx, gy + 1 - 2 * core)
    level_devices = (
        [],
        [to_x[0]],
        [to_z_high],
        to_y,
        [to_y[0]],
        [to_z_low],
        [to_core],
    )
    level_picks = (
        (0,),
        (x % 2, 1 - x % 2),
        (z_high, 1 - z_high),
        y_flips,
        (y % 2, 1 - y % 2),
        (z_low, 1 - z_low),
        (core, 1 - core),
    )
    stage_devices = (to_x, [to_z_high], to_y, [to_z_low], [to_core])
    stage_picks = (x_flips, (z_high, 1 - z_high), y_flips, (z_low, 1 - z_low), (core, 1 - core))
    greeted = to_x + to_y + [to_z_high, to_z_low, to_core]

    barrier = pltpu.get_barrier_semaphore()
    for device in greeted:
        pl.semaphore_signal(barrier, inc=1, device_id=device, device_id_type=MESH)

    def weight_copy(unit):
        return pltpu.make_async_copy(w_ref.at[:, unit], w_buf.at[unit], w_sem.at[unit])

    def phase_part(level, pick, unit):
        return p_refs[level].at[level, pl.ds(pick * PICKED[level], PICKED[level]), unit]

    def phase_copy(level, unit):
        return pltpu.make_async_copy(
            phase_part(level, level_picks[level][0], unit),
            p_bufs[level].at[0, unit],
            p_sem.at[level, unit % LOCAL_SLOTS],
        )

    def phase_send(level, j, unit):
        lane = level + j - 1 + (2 if level > 3 else 0) - 1
        return pltpu.make_async_remote_copy(
            src_ref=phase_part(level, level_picks[level][j], unit),
            dst_ref=p_bufs[level].at[j, unit],
            send_sem=give_sem.at[lane, unit % STATIC_SLOTS],
            recv_sem=get_sem.at[lane, unit],
            device_id=level_devices[level][j - 1],
            device_id_type=MESH,
        )

    def held_part(stage, slot, j):
        pick = stage_picks[stage][j]
        if stage == 2:
            return held[stage].at[slot, :, pl.ds(pick * 4 * LOW, 4 * LOW)]
        if stage == 4:
            return held[stage].at[slot, :, pl.ds(pick * 8 * LOW, 8 * LOW)]
        return held[stage].at[slot, pick]

    def exchange(stage, j, chunk):
        slot = chunk % SLOTS
        lane = sum(PARTNERS[:stage]) + j - 1
        return pltpu.make_async_remote_copy(
            src_ref=held_part(stage, slot, j),
            dst_ref=came[stage].at[j - 1, chunk],
            send_sem=send_sem.at[lane, slot],
            recv_sem=recv_sem.at[lane, chunk],
            device_id=stage_devices[stage][j - 1],
            device_id_type=MESH,
        )

    def out_copy(chunk):
        return pltpu.make_async_copy(
            staged.at[chunk], out_ref.at[pl.ds(chunk * 2 * ROWS, 2 * ROWS)], out_sem.at[chunk]
        )

    def phase_rows(level, box, chunk, offset, count, stride):
        per = chunks_per_unit(level)
        flat = p_bufs[level].at[box, chunk // per].reshape(PICKED[level] * unit_rows(level), 128)
        start = (chunk % per) * (1 << low_bits(level)) + offset if per > 1 else offset
        return flat[pl.ds(start, count, stride=stride)]

    def keep(stage, slot, halves, start, real, imag):
        size = real.shape[0] // halves
        for half in range(halves):
            for part, value in enumerate((real, imag)):
                held[stage][slot, half, part, pl.ds(start, size)] = value[half * size : half * size + size]

    def own_and_came(stage, chunk):
        own = held_part(stage, chunk % SLOTS, 0)
        blocks = [own[0], own[1]]
        for j in range(PARTNERS[stage]):
            blocks += [came[stage][j, chunk, 0], came[stage][j, chunk, 1]]
        return blocks

    def first_stage(chunk):
        per = chunks_per_unit(0)
        slot = chunk % SLOTS
        flat = w_buf.at[chunk // per].reshape(128 * 16, 128)
        left = lax.broadcasted_iota(jnp.int32, (32, 128), 1) < 64
        for u in range(1 << low_bits(0)):
            row = (chunk % per) * (1 << low_bits(0)) + u
            for quarter in range(4):
                even = flat[pl.ds(quarter * 32 * 16 + 2 * row, 32, stride=16)]
                odd = flat[pl.ds(quarter * 32 * 16 + 2 * row + 1, 32, stride=16)]
                real = jnp.where(left, even, pltpu.roll(odd, 64, 1))
                imag = jnp.where(left, pltpu.roll(even, 64, 1), odd)
                angle = phase_rows(0, 0, chunk, quarter * 32 * 8 + u, 32, 8)
                real, imag = turned(real, imag, angle)
                held[0][slot, quarter, 0, pl.ds(u * 32, 32)] = real
                held[0][slot, quarter, 1, pl.ds(u * 32, 32)] = imag

    def pair_sum(out, size, rows, lanes, angles):
        total = None
        for box, angle in enumerate(angles):
            start = box * 2 * size + rows.start
            real = out[start : start + rows.stop - rows.start, lanes]
            imag = out[start + size : start + size + rows.stop - rows.start, lanes]
            value = turned(real, imag, angle)
            total = value if total is None else (total[0] + value[0], total[1] + value[1])
        return total

    def sides():
        return [(i, slice(i * 128, i * 128 + 128)) for i in range(2)]

    def second_stage(chunk):
        b = own_and_came(0, chunk)
        blocks = [b[0] + b[4], b[1] + b[5], b[2] + b[6], b[3] + b[7]]
        out = stacked_dot(blocks, mats_ref, 0)
        for u in range(LOW // 4):
            for i, lanes in sides():
                angles = [phase_rows(1, box, chunk, 2 * u + i, 32, 8) for box in range(2)]
                real, imag = pair_sum(out, HALF // 2, slice(u * 32, u * 32 + 32), lanes, angles)
                keep(1, chunk % SLOTS, 2, (2 * u + i) * 16, real, imag)

    def third_stage(chunk):
        out = stacked_dot(own_and_came(1, chunk), mats_ref, 0)
        for u in range(LOW // 2):
            for i, lanes in sides():
                angles = [phase_rows(2, box, chunk, 2 * u + i, 16, 8) for box in range(2)]
                sums = pair_sum(out, HALF // 2, slice(u * 16, u * 16 + 16), lanes, angles)
                for part in range(2):
                    held[2].at[chunk % SLOTS, part][pl.ds(2 * u + i, 16, stride=LOW)] = sums[part]

    def fourth_stage(chunk):
        size = 4 * LOW
        out = stacked_dot(own_and_came(2, chunk), mats_ref, 0)
        blocks = []
        for pair in range(2):
            parts = ([], [])
            for i, lanes in sides():
                total = None
                for box in (pair, pair + 2):
                    angle = phase_rows(3, box, chunk, i, size, 2)
                    start = box * 2 * size
                    value = turned(out[start : start + size, lanes], out[start + size : start + 2 * size, lanes], angle)
                    total = value if total is None else (total[0] + value[0], total[1] + value[1])
                parts[0].append(total[0])
                parts[1].append(total[1])
            blocks += [jnp.concatenate(p, axis=0) for p in parts]
        out = stacked_dot(blocks, mats_ref, 1)
        for i in range(2):
            for k, lanes in sides():
                angles = [phase_rows(4, box, chunk, 2 * i + k, size, 4) for box in range(2)]
                real, imag = pair_sum(out, 2 * size, slice(i * size, i * size + size), lanes, angles)
                keep(3, chunk % SLOTS, 2, (2 * i + k) * 2 * LOW, real, imag)

    def fifth_stage(chunk):
        size = 2 * LOW
        out = stacked_dot(own_and_came(3, chunk), mats_ref, 1)
        for low in range(4):
            for m, lanes in sides():
                angles = [phase_rows(5, box, chunk, 2 * low + m, size, 8) for box in range(2)]
                sums = pair_sum(out, 4 * size, slice(low * size, low * size + size), lanes, angles)
                for part in range(2):
                    held[4].at[chunk % SLOTS, part][pl.ds(2 * low + m, size, stride=8)] = sums[part]

    def last_stage(chunk):
        size = 8 * LOW
        out = stacked_dot(own_and_came(4, chunk), mats_ref, 1)
        rows = []
        for n, lanes in sides():
            angles = [phase_rows(6, box, chunk, n, size, 2) for box in range(2)]
            rows.append(jnp.concatenate(pair_sum(out, size, slice(0, size), lanes, angles), axis=1))
        high, low = split_value(jnp.concatenate(rows, axis=0))
        out = dot(high, last_ref[0]) + dot(low, last_ref[0]) + dot(high, last_ref[1])
        for n in range(2):
            for k in range(4):
                staged.at[chunk][pl.ds(n * 4 + k, size, stride=8)] = out[
                    n * size : n * size + size, k * 128 : k * 128 + 128
                ]

    stage_bodies = (first_stage, second_stage, third_stage, fourth_stage, fifth_stage, last_stage)

    def fetch(time):
        for level in range(LEVELS):
            ahead = time + AHEAD - STAGE_OF[level] * DEPTH
            per = chunks_per_unit(level)

            @pl.when((ahead >= 0) & (ahead < CHUNKS) & (ahead % per == 0))
            def _():
                phase_copy(level, ahead // per).start()
                if level == 0:
                    weight_copy(ahead // per).start()

    def give(time):
        for level in range(1, LEVELS):
            chunk = time - SEND_AT[level]
            per = chunks_per_unit(level)

            @pl.when((chunk >= 0) & (chunk < CHUNKS) & (chunk % per == 0))
            def _():
                unit = chunk // per

                @pl.when(unit >= STATIC_SLOTS)
                def _():
                    for j in range(1, BOXES[level]):
                        phase_send(level, j, unit - STATIC_SLOTS).wait_send()

                for j in range(1, BOXES[level]):
                    phase_send(level, j, unit).start()

    def work(time):
        for stage in range(STAGES):
            chunk = time - stage * DEPTH

            @pl.when((chunk >= 0) & (chunk < CHUNKS))
            def _():
                for level in range(LEVELS):
                    if STAGE_OF[level] == stage:
                        per = chunks_per_unit(level)

                        @pl.when(chunk % per == 0)
                        def _():
                            phase_copy(level, chunk // per).wait()
                            if level == 0:
                                weight_copy(chunk // per).wait()
                            for j in range(1, BOXES[level]):
                                phase_send(level, j, chunk // per).wait_recv()

                if stage > 0:
                    for j in range(1, PARTNERS[stage - 1] + 1):
                        exchange(stage - 1, j, chunk).wait_recv()
                if stage < STAGES - 1:

                    @pl.when(chunk >= SLOTS)
                    def _():
                        for j in range(1, PARTNERS[stage] + 1):
                            exchange(stage, j, chunk - SLOTS).wait_send()

                stage_bodies[stage](chunk)
                if stage < STAGES - 1:
                    for j in range(1, PARTNERS[stage] + 1):
                        exchange(stage, j, chunk).start()
                else:
                    out_copy(chunk).start()

    def early(time, carry):
        fetch(time)
        return carry

    lax.fori_loop(-AHEAD, 0, early, 0)
    pl.semaphore_wait(barrier, len(greeted))

    def step(time, carry):
        fetch(time)
        give(time)
        work(time)
        return carry

    lax.fori_loop(0, CHUNKS + (STAGES - 1) * DEPTH, step, 0)

    def finish(chunk, carry):
        for stage in range(STAGES - 1):
            for j in range(1, PARTNERS[stage] + 1):
                exchange(stage, j, chunk).wait_send()
        return carry

    lax.fori_loop(CHUNKS - SLOTS, CHUNKS, finish, 0)
    for level in range(1, LEVELS):

        def given(unit, carry):
            for j in range(1, BOXES[level]):
                phase_send(level, j, unit).wait_send()
            return carry

        lax.fori_loop(units(level) - STATIC_SLOTS, units(level), given, 0)

    def drain(chunk, carry):
        out_copy(chunk).wait()
        return carry

    lax.fori_loop(0, CHUNKS, drain, 0)


def shards(weights, phases):
    mats, last = refine_matrices()
    views = [
        phases.reshape(LEVELS, sel_count(level), units(level), unit_rows(level), 128)
        for level in range(LEVELS)
    ]
    anywhere = pl.BlockSpec(memory_space=pl.ANY)
    vmem = pl.BlockSpec(memory_space=pltpu.VMEM)

    def buffer(*shape):
        return pltpu.VMEM(shape + (128,), jnp.float32)

    scratch = [buffer(4, 128, 16)]
    scratch += [
        buffer(BOXES[level], units(level), PICKED[level], unit_rows(level)) for level in range(LEVELS)
    ]
    scratch += [
        buffer(SLOTS, 4, 2, HALF // 2),
        buffer(SLOTS, 2, 2, HALF // 2),
        buffer(SLOTS, 2, HALF),
        buffer(SLOTS, 2, 2, HALF // 2),
        buffer(SLOTS, 2, HALF),
    ]
    scratch += [
        buffer(3, CHUNKS, 2, HALF // 2),
        buffer(1, CHUNKS, 2, HALF // 2),
        buffer(3, CHUNKS, 2, HALF // 4),
        buffer(1, CHUNKS, 2, HALF // 2),
        buffer(1, CHUNKS, 2, HALF // 2),
    ]
    scratch += [
        buffer(CHUNKS, 2 * ROWS),
        pltpu.SemaphoreType.DMA((4,)),
        pltpu.SemaphoreType.DMA((LEVELS, LOCAL_SLOTS)),
        pltpu.SemaphoreType.DMA((8, STATIC_SLOTS)),
        pltpu.SemaphoreType.DMA((8, CHUNKS)),
        pltpu.SemaphoreType.DMA((9, SLOTS)),
        pltpu.SemaphoreType.DMA((9, CHUNKS)),
        pltpu.SemaphoreType.DMA((CHUNKS,)),
    ]
    return pl.pallas_call(
        kernel,
        out_shape=jax.ShapeDtypeStruct(weights.shape, jnp.float32),
        in_specs=[anywhere] * (LEVELS + 1) + [vmem] * 2,
        out_specs=anywhere,
        scratch_shapes=scratch,
        compiler_params=pltpu.CompilerParams(
            collective_id=0, has_side_effects=True, vmem_limit_bytes=58 * 2**20
        ),
    )(weights.reshape(128, 4, 16, 128), *views, jnp.asarray(mats), jnp.asarray(last))


def solution(mesh):
    return jax.shard_map(
        shards,
        mesh=mesh,
        in_specs=(P(("gx", "gy"), None), P(None, ("gx", "gy"), None)),
        out_specs=P(("gx", "gy"), None),
        check_vma=False,
    )
```

```python
import functools
import math

import jax
import jax.numpy as jnp
import numpy as np
from jax import lax
from jax.experimental import pallas as pl
from jax.experimental.pallas import tpu as pltpu
from jax.sharding import PartitionSpec as P

MESH = pl.DeviceIdType.MESH
LEVELS = 7
CHUNK_BITS = 3
CHUNKS = 1 << CHUNK_BITS
ROWS = 4096 // CHUNKS
HALF = ROWS // 2
LOW = 1 << (7 - CHUNK_BITS)
STAGES = 6
OFFSETS = (0, 2, 4, 6, 8, 9)
SLOTS = 4
AHEAD = 3
LOCAL_SLOTS = 4
STATIC_SLOTS = 4
BOXES = (1, 2, 2, 4, 2, 2, 2)
PICKED = (128, 32, 16, 4, 4, 2, 1)
STAGE_OF = (0, 1, 2, 3, 3, 4, 5)
SEND_AT = (0, 0, 0, 0, 0, 0, 0)
PARTNERS = (3, 1, 3, 1, 1)


def low_bits(level):
    return 5 - CHUNK_BITS + level


def unit_rows(level):
    return max(8, 1 << low_bits(level))


def units(level):
    return (1 << (5 + level)) // unit_rows(level)


def sel_count(level):
    return 1 << (7 - level)


def chunks_per_unit(level):
    return CHUNKS // units(level)


def series(func, degree):
    top = 3.140625**2
    nodes = (np.cos((np.arange(64) + 0.5) * np.pi / 64) + 1.0) * top / 2
    fit = np.polynomial.chebyshev.Chebyshev.fit(nodes, func(np.sqrt(nodes)), degree, domain=[0.0, top])
    return [float(np.float32(c)) for c in fit.convert(kind=np.polynomial.Polynomial).coef]


COS_COEF = series(np.cos, 6)
SIN_COEF = series(lambda r: np.sin(r) / r, 5)


def horner(coef, square):
    total = jnp.full_like(square, coef[-1])
    total = coef[-1] * square + coef[-2]
    for c in reversed(coef[:-2]):
        total = total * square + c
    return total


def cos_sin(angle):
    square = angle * angle
    return horner(COS_COEF, square), horner(SIN_COEF, square) * angle


def refine_matrices():
    nodes = np.cos((2.0 * np.arange(8) + 1.0) * math.pi / 16.0)
    sides = []
    for child in range(2):
        points = (nodes + 2.0 * child - 1.0) / 2.0
        lagrange = np.ones((8, 8))
        for j in range(8):
            for m in range(8):
                if m != j:
                    lagrange[j] *= (points - nodes[m]) / (nodes[j] - nodes[m])
        sides.append(lagrange)
    eye = np.eye(8)
    first = np.concatenate([np.kron(k, eye) for k in sides], axis=1)
    second = np.concatenate([np.kron(eye, k) for k in sides], axis=1)
    zero = np.zeros_like(first)

    def split(matrix):
        matrix = np.asarray(matrix, np.float32)
        high = matrix.astype(jnp.bfloat16)
        low = (matrix - high.astype(np.float32)).astype(jnp.bfloat16)
        return high, low

    mats = []
    for pair in (first, second):
        high, low = split(np.block([[pair, zero], [zero, pair]]))
        mats.append(np.stack([np.concatenate([high, high]), np.concatenate([low, low])]))
    last = np.zeros((256, 512))
    for slot in range(2):
        for child in range(2):
            edge = second[:, 64 * child : 64 * child + 64]
            col = 256 * slot + 128 * child
            last[64 * slot : 64 * slot + 64, col : col + 64] = edge
            last[128 + 64 * slot : 192 + 64 * slot, col + 64 : col + 128] = edge
    high, low = split(last)
    return np.stack(mats), np.stack([high, low])


def split_value(x):
    high = x.astype(jnp.bfloat16)
    low = (x - high.astype(jnp.float32)).astype(jnp.bfloat16)
    return high, low


def stacked_dot(blocks, mats, which):
    high, low = split_value(jnp.concatenate(blocks, axis=0))
    wide = jnp.concatenate([high, low], axis=1)
    return dot(wide, mats[which, 0]) + dot(wide, mats[which, 1])


def turned(real, imag, angle):
    cosine, sine = cos_sin(angle)
    return cosine * real - sine * imag, sine * real + cosine * imag


def dot(a, b):
    return jnp.dot(a, b, preferred_element_type=jnp.float32)


def kernel(w_ref, *refs):
    p_refs = refs[:LEVELS]
    mats_ref, last_ref, out_ref = refs[LEVELS : LEVELS + 3]
    w_buf = refs[LEVELS + 3]
    p_bufs = refs[LEVELS + 4 : 2 * LEVELS + 4]
    held = refs[2 * LEVELS + 4 : 2 * LEVELS + 9]
    came = refs[2 * LEVELS + 9 : 2 * LEVELS + 14]
    staged, w_sem, p_sem, give_sem, get_sem, send_sem, recv_sem, out_sem = refs[2 * LEVELS + 14 :]

    gx = lax.axis_index("gx")
    gy = lax.axis_index("gy")
    x, z_high = gx // 2, gx % 2
    y, z_low, core = gy // 4, (gy // 2) % 2, gy % 2

    def flips(v):
        return (v, v + 1 - 2 * (v % 2), (v + 2) % 4, 3 - v)

    x_flips = flips(x)
    y_flips = flips(y)
    to_x = [(x_flips[j] * 2 + z_high, gy) for j in range(1, 4)]
    to_z_high = (gx + 1 - 2 * z_high, gy)
    to_y = [(gx, y_flips[j] * 4 + z_low * 2 + core) for j in range(1, 4)]
    to_z_low = (gx, gy + 2 - 4 * z_low)
    to_core = (gx, gy + 1 - 2 * core)
    level_devices = (
        [],
        [to_x[0]],
        [to_z_high],
        to_y,
        [to_y[0]],
        [to_z_low],
        [to_core],
    )
    level_picks = (
        (0,),
        (x % 2, 1 - x % 2),
        (z_high, 1 - z_high),
        y_flips,
        (y % 2, 1 - y % 2),
        (z_low, 1 - z_low),
        (core, 1 - core),
    )
    stage_devices = (to_x, [to_z_high], to_y, [to_z_low], [to_core])
    stage_picks = (x_flips, (z_high, 1 - z_high), y_flips, (z_low, 1 - z_low), (core, 1 - core))
    greeted = to_x + to_y + [to_z_high, to_z_low, to_core]

    barrier = pltpu.get_barrier_semaphore()
    for device in greeted:
        pl.semaphore_signal(barrier, inc=1, device_id=device, device_id_type=MESH)

    def weight_copy(unit):
        return pltpu.make_async_copy(w_ref.at[:, unit], w_buf.at[unit], w_sem.at[unit])

    def phase_part(level, pick, unit):
        return p_refs[level].at[level, pl.ds(pick * PICKED[level], PICKED[level]), unit]

    def phase_copy(level, unit):
        return pltpu.make_async_copy(
            phase_part(level, level_picks[level][0], unit),
            p_bufs[level].at[0, unit],
            p_sem.at[level, unit % LOCAL_SLOTS],
        )

    def phase_send(level, j, unit):
        lane = level + j - 1 + (2 if level > 3 else 0) - 1
        return pltpu.make_async_remote_copy(
            src_ref=phase_part(level, level_picks[level][j], unit),
            dst_ref=p_bufs[level].at[j, unit],
            send_sem=give_sem.at[lane, unit % STATIC_SLOTS],
            recv_sem=get_sem.at[lane, unit],
            device_id=level_devices[level][j - 1],
            device_id_type=MESH,
        )

    def held_part(stage, slot, j):
        pick = stage_picks[stage][j]
        if stage == 2:
            return held[stage].at[slot, :, pl.ds(pick * 4 * LOW, 4 * LOW)]
        if stage == 4:
            return held[stage].at[slot, :, pl.ds(pick * 8 * LOW, 8 * LOW)]
        return held[stage].at[slot, pick]

    def exchange(stage, j, chunk):
        slot = chunk % SLOTS
        lane = sum(PARTNERS[:stage]) + j - 1
        return pltpu.make_async_remote_copy(
            src_ref=held_part(stage, slot, j),
            dst_ref=came[stage].at[j - 1, chunk],
            send_sem=send_sem.at[lane, slot],
            recv_sem=recv_sem.at[lane, chunk],
            device_id=stage_devices[stage][j - 1],
            device_id_type=MESH,
        )

    def out_copy(chunk):
        return pltpu.make_async_copy(
            staged.at[chunk], out_ref.at[pl.ds(chunk * 2 * ROWS, 2 * ROWS)], out_sem.at[chunk]
        )

    def phase_rows(level, box, chunk, offset, count, stride):
        per = chunks_per_unit(level)
        flat = p_bufs[level].at[box, chunk // per].reshape(PICKED[level] * unit_rows(level), 128)
        start = (chunk % per) * (1 << low_bits(level)) + offset if per > 1 else offset
        return flat[pl.ds(start, count, stride=stride)]

    def keep(stage, slot, halves, start, real, imag):
        size = real.shape[0] // halves
        for half in range(halves):
            for part, value in enumerate((real, imag)):
                held[stage][slot, half, part, pl.ds(start, size)] = value[half * size : half * size + size]

    def own_and_came(stage, chunk):
        own = held_part(stage, chunk % SLOTS, 0)
        blocks = [own[0], own[1]]
        for j in range(PARTNERS[stage]):
            blocks += [came[stage][j, chunk, 0], came[stage][j, chunk, 1]]
        return blocks

    def first_stage(chunk):
        per = chunks_per_unit(0)
        slot = chunk % SLOTS
        flat = w_buf.at[chunk // per].reshape(128 * 16, 128)
        left = lax.broadcasted_iota(jnp.int32, (32, 128), 1) < 64
        for u in range(1 << low_bits(0)):
            row = (chunk % per) * (1 << low_bits(0)) + u
            for quarter in range(4):
                even = flat[pl.ds(quarter * 32 * 16 + 2 * row, 32, stride=16)]
                odd = flat[pl.ds(quarter * 32 * 16 + 2 * row + 1, 32, stride=16)]
                real = jnp.where(left, even, pltpu.roll(odd, 64, 1))
                imag = jnp.where(left, pltpu.roll(even, 64, 1), odd)
                angle = phase_rows(0, 0, chunk, quarter * 32 * 8 + u, 32, 8)
                real, imag = turned(real, imag, angle)
                held[0][slot, quarter, 0, pl.ds(u * 32, 32)] = real
                held[0][slot, quarter, 1, pl.ds(u * 32, 32)] = imag

    def pair_sum(out, size, rows, lanes, angles):
        total = None
        for box, angle in enumerate(angles):
            start = box * 2 * size + rows.start
            real = out[start : start + rows.stop - rows.start, lanes]
            imag = out[start + size : start + size + rows.stop - rows.start, lanes]
            value = turned(real, imag, angle)
            total = value if total is None else (total[0] + value[0], total[1] + value[1])
        return total

    def sides():
        return [(i, slice(i * 128, i * 128 + 128)) for i in range(2)]

    def second_stage(chunk):
        b = own_and_came(0, chunk)
        blocks = [b[0] + b[4], b[1] + b[5], b[2] + b[6], b[3] + b[7]]
        out = stacked_dot(blocks, mats_ref, 0)
        for u in range(LOW // 4):
            for i, lanes in sides():
                angles = [phase_rows(1, box, chunk, 2 * u + i, 32, unit_rows(1)) for box in range(2)]
                real, imag = pair_sum(out, HALF // 2, slice(u * 32, u * 32 + 32), lanes, angles)
                keep(1, chunk % SLOTS, 2, (2 * u + i) * 16, real, imag)

    def third_stage(chunk):
        out = stacked_dot(own_and_came(1, chunk), mats_ref, 0)
        for u in range(LOW // 2):
            for i, lanes in sides():
                angles = [phase_rows(2, box, chunk, 2 * u + i, 16, unit_rows(2)) for box in range(2)]
                sums = pair_sum(out, HALF // 2, slice(u * 16, u * 16 + 16), lanes, angles)
                for part in range(2):
                    held[2].at[chunk % SLOTS, part][pl.ds(2 * u + i, 16, stride=LOW)] = sums[part]

    def fourth_stage(chunk):
        size = 4 * LOW
        out = stacked_dot(own_and_came(2, chunk), mats_ref, 0)
        blocks = []
        for pair in range(2):
            parts = ([], [])
            for i, lanes in sides():
                total = None
                for box in (pair, pair + 2):
                    angle = phase_rows(3, box, chunk, i, size, 2)
                    start = box * 2 * size
                    value = turned(out[start : start + size, lanes], out[start + size : start + 2 * size, lanes], angle)
                    total = value if total is None else (total[0] + value[0], total[1] + value[1])
                parts[0].append(total[0])
                parts[1].append(total[1])
            blocks += [jnp.concatenate(p, axis=0) for p in parts]
        out = stacked_dot(blocks, mats_ref, 1)
        for i in range(2):
            for k, lanes in sides():
                angles = [phase_rows(4, box, chunk, 2 * i + k, size, 4) for box in range(2)]
                real, imag = pair_sum(out, 2 * size, slice(i * size, i * size + size), lanes, angles)
                keep(3, chunk % SLOTS, 2, (2 * i + k) * 2 * LOW, real, imag)

    def fifth_stage(chunk):
        size = 2 * LOW
        out = stacked_dot(own_and_came(3, chunk), mats_ref, 1)
        for low in range(4):
            for m, lanes in sides():
                angles = [phase_rows(5, box, chunk, 2 * low + m, size, 8) for box in range(2)]
                sums = pair_sum(out, 4 * size, slice(low * size, low * size + size), lanes, angles)
                for part in range(2):
                    held[4].at[chunk % SLOTS, part][pl.ds(2 * low + m, size, stride=8)] = sums[part]

    def last_stage(chunk):
        size = 8 * LOW
        out = stacked_dot(own_and_came(4, chunk), mats_ref, 1)
        rows = []
        for n, lanes in sides():
            angles = [phase_rows(6, box, chunk, n, size, 2) for box in range(2)]
            rows.append(jnp.concatenate(pair_sum(out, size, slice(0, size), lanes, angles), axis=1))
        high, low = split_value(jnp.concatenate(rows, axis=0))
        out = dot(high, last_ref[0]) + dot(low, last_ref[0]) + dot(high, last_ref[1])
        for n in range(2):
            for k in range(4):
                staged.at[chunk][pl.ds(n * 4 + k, size, stride=8)] = out[
                    n * size : n * size + size, k * 128 : k * 128 + 128
                ]

    stage_bodies = (first_stage, second_stage, third_stage, fourth_stage, fifth_stage, last_stage)

    def fetch(time):
        for level in range(LEVELS):
            ahead = time + AHEAD - OFFSETS[STAGE_OF[level]]
            per = chunks_per_unit(level)

            @pl.when((ahead >= 0) & (ahead < CHUNKS) & (ahead % per == 0))
            def _():
                phase_copy(level, ahead // per).start()
                if level == 0:
                    weight_copy(ahead // per).start()

    def give(time):
        for level in range(1, LEVELS):
            chunk = time - SEND_AT[level]
            per = chunks_per_unit(level)

            @pl.when((chunk >= 0) & (chunk < CHUNKS) & (chunk % per == 0))
            def _():
                unit = chunk // per

                @pl.when(unit >= STATIC_SLOTS)
                def _():
                    for j in range(1, BOXES[level]):
                        phase_send(level, j, unit - STATIC_SLOTS).wait_send()

                for j in range(1, BOXES[level]):
                    phase_send(level, j, unit).start()

    def work(time):
        for stage in range(STAGES):
            chunk = time - OFFSETS[stage]

            @pl.when((chunk >= 0) & (chunk < CHUNKS))
            def _():
                for level in range(LEVELS):
                    if STAGE_OF[level] == stage:
                        per = chunks_per_unit(level)

                        @pl.when(chunk % per == 0)
                        def _():
                            phase_copy(level, chunk // per).wait()
                            if level == 0:
                                weight_copy(chunk // per).wait()
                            for j in range(1, BOXES[level]):
                                phase_send(level, j, chunk // per).wait_recv()

                if stage > 0:
                    for j in range(1, PARTNERS[stage - 1] + 1):
                        exchange(stage - 1, j, chunk).wait_recv()
                if stage < STAGES - 1:

                    @pl.when(chunk >= SLOTS)
                    def _():
                        for j in range(1, PARTNERS[stage] + 1):
                            exchange(stage, j, chunk - SLOTS).wait_send()

                stage_bodies[stage](chunk)
                if stage < STAGES - 1:
                    for j in range(1, PARTNERS[stage] + 1):
                        exchange(stage, j, chunk).start()
                else:
                    out_copy(chunk).start()

    def early(time, carry):
        fetch(time)
        return carry

    lax.fori_loop(-AHEAD, 0, early, 0)
    pl.semaphore_wait(barrier, len(greeted))

    def lead(time, carry):
        give(time)
        return carry

    lax.fori_loop(min(SEND_AT), 0, lead, 0)

    def step(time, carry):
        fetch(time)
        give(time)
        work(time)
        return carry

    lax.fori_loop(0, CHUNKS + OFFSETS[-1], step, 0)

    def finish(chunk, carry):
        for stage in range(STAGES - 1):
            for j in range(1, PARTNERS[stage] + 1):
                exchange(stage, j, chunk).wait_send()
        return carry

    lax.fori_loop(CHUNKS - SLOTS, CHUNKS, finish, 0)
    for level in range(1, LEVELS):

        def given(unit, carry):
            for j in range(1, BOXES[level]):
                phase_send(level, j, unit).wait_send()
            return carry

        lax.fori_loop(units(level) - STATIC_SLOTS, units(level), given, 0)

    def drain(chunk, carry):
        out_copy(chunk).wait()
        return carry

    lax.fori_loop(0, CHUNKS, drain, 0)


def shards(weights, phases):
    mats, last = refine_matrices()
    views = [
        phases.reshape(LEVELS, sel_count(level), units(level), unit_rows(level), 128)
        for level in range(LEVELS)
    ]
    anywhere = pl.BlockSpec(memory_space=pl.ANY)
    vmem = pl.BlockSpec(memory_space=pltpu.VMEM)

    def buffer(*shape):
        return pltpu.VMEM(shape + (128,), jnp.float32)

    scratch = [buffer(4, 128, 16)]
    scratch += [
        buffer(BOXES[level], units(level), PICKED[level], unit_rows(level)) for level in range(LEVELS)
    ]
    scratch += [
        buffer(SLOTS, 4, 2, HALF // 2),
        buffer(SLOTS, 2, 2, HALF // 2),
        buffer(SLOTS, 2, HALF),
        buffer(SLOTS, 2, 2, HALF // 2),
        buffer(SLOTS, 2, HALF),
    ]
    scratch += [
        buffer(3, CHUNKS, 2, HALF // 2),
        buffer(1, CHUNKS, 2, HALF // 2),
        buffer(3, CHUNKS, 2, HALF // 4),
        buffer(1, CHUNKS, 2, HALF // 2),
        buffer(1, CHUNKS, 2, HALF // 2),
    ]
    scratch += [
        buffer(CHUNKS, 2 * ROWS),
        pltpu.SemaphoreType.DMA((4,)),
        pltpu.SemaphoreType.DMA((LEVELS, LOCAL_SLOTS)),
        pltpu.SemaphoreType.DMA((8, STATIC_SLOTS)),
        pltpu.SemaphoreType.DMA((8, CHUNKS)),
        pltpu.SemaphoreType.DMA((9, SLOTS)),
        pltpu.SemaphoreType.DMA((9, CHUNKS)),
        pltpu.SemaphoreType.DMA((CHUNKS,)),
    ]
    return pl.pallas_call(
        kernel,
        out_shape=jax.ShapeDtypeStruct(weights.shape, jnp.float32),
        in_specs=[anywhere] * (LEVELS + 1) + [vmem] * 2,
        out_specs=anywhere,
        scratch_shapes=scratch,
        compiler_params=pltpu.CompilerParams(
            collective_id=0, has_side_effects=True, vmem_limit_bytes=58 * 2**20
        ),
    )(weights.reshape(128, 4, 16, 128), *views, jnp.asarray(mats), jnp.asarray(last))


def solution(mesh):
    return jax.shard_map(
        shards,
        mesh=mesh,
        in_specs=(P(("gx", "gy"), None), P(None, ("gx", "gy"), None)),
        out_specs=P(("gx", "gy"), None),
        check_vma=False,
    )
```

```python
import functools
import math

import jax
import jax.numpy as jnp
import numpy as np
from jax import lax
from jax.experimental import pallas as pl
from jax.experimental.pallas import tpu as pltpu
from jax.sharding import PartitionSpec as P

MESH = pl.DeviceIdType.MESH
LEVELS = 7
CHUNK_BITS = 3
CHUNKS = 1 << CHUNK_BITS
ROWS = 4096 // CHUNKS
HALF = ROWS // 2
LOW = 1 << (7 - CHUNK_BITS)
STAGES = 6
OFFSETS = (0, 2, 4, 6, 8, 9)
SLOTS = 4
AHEAD = 3
PIECES = 8
LOCAL_SLOTS = 4
STATIC_SLOTS = 4
BOXES = (1, 2, 2, 4, 2, 2, 2)
PICKED = (128, 32, 16, 4, 4, 2, 1)
STAGE_OF = (0, 1, 2, 3, 3, 4, 5)
SEND_AT = (0, 0, 0, 0, 0, 0, 0)
PARTNERS = (3, 1, 3, 1, 1)


def low_bits(level):
    return 5 - CHUNK_BITS + level


def unit_rows(level):
    return max(8, 1 << low_bits(level))


def units(level):
    return (1 << (5 + level)) // unit_rows(level)


def sel_count(level):
    return 1 << (7 - level)


def chunks_per_unit(level):
    return CHUNKS // units(level)


def series(func, degree):
    top = 3.140625**2
    nodes = (np.cos((np.arange(64) + 0.5) * np.pi / 64) + 1.0) * top / 2
    fit = np.polynomial.chebyshev.Chebyshev.fit(nodes, func(np.sqrt(nodes)), degree, domain=[0.0, top])
    return [float(np.float32(c)) for c in fit.convert(kind=np.polynomial.Polynomial).coef]


COS_COEF = series(np.cos, 6)
SIN_COEF = series(lambda r: np.sin(r) / r, 5)


def horner(coef, square):
    total = jnp.full_like(square, coef[-1])
    total = coef[-1] * square + coef[-2]
    for c in reversed(coef[:-2]):
        total = total * square + c
    return total


def cos_sin(angle):
    square = angle * angle
    return horner(COS_COEF, square), horner(SIN_COEF, square) * angle


def refine_matrices():
    nodes = np.cos((2.0 * np.arange(8) + 1.0) * math.pi / 16.0)
    sides = []
    for child in range(2):
        points = (nodes + 2.0 * child - 1.0) / 2.0
        lagrange = np.ones((8, 8))
        for j in range(8):
            for m in range(8):
                if m != j:
                    lagrange[j] *= (points - nodes[m]) / (nodes[j] - nodes[m])
        sides.append(lagrange)
    eye = np.eye(8)
    first = np.concatenate([np.kron(k, eye) for k in sides], axis=1)
    second = np.concatenate([np.kron(eye, k) for k in sides], axis=1)
    zero = np.zeros_like(first)

    def split(matrix):
        matrix = np.asarray(matrix, np.float32)
        high = matrix.astype(jnp.bfloat16)
        low = (matrix - high.astype(np.float32)).astype(jnp.bfloat16)
        return high, low

    mats = []
    for pair in (first, second):
        high, low = split(np.block([[pair, zero], [zero, pair]]))
        mats.append(np.stack([np.concatenate([high, high]), np.concatenate([low, low])]))
    last = np.zeros((256, 512))
    for slot in range(2):
        for child in range(2):
            edge = second[:, 64 * child : 64 * child + 64]
            col = 256 * slot + 128 * child
            last[64 * slot : 64 * slot + 64, col : col + 64] = edge
            last[128 + 64 * slot : 192 + 64 * slot, col + 64 : col + 128] = edge
    high, low = split(last)
    return np.stack(mats), np.stack([high, low])


def split_value(x):
    high = x.astype(jnp.bfloat16)
    low = (x - high.astype(jnp.float32)).astype(jnp.bfloat16)
    return high, low


def stacked_dot(blocks, mats, which):
    high, low = split_value(jnp.concatenate(blocks, axis=0))
    wide = jnp.concatenate([high, low], axis=1)
    return dot(wide, mats[which, 0]) + dot(wide, mats[which, 1])


def turned(real, imag, angle):
    cosine, sine = cos_sin(angle)
    return cosine * real - sine * imag, sine * real + cosine * imag


def dot(a, b):
    return jnp.dot(a, b, preferred_element_type=jnp.float32)


def kernel(w_ref, *refs):
    p_refs = refs[:LEVELS]
    mats_ref, last_ref, out_ref = refs[LEVELS : LEVELS + 3]
    w_buf = refs[LEVELS + 3]
    p_bufs = refs[LEVELS + 4 : 2 * LEVELS + 4]
    held = refs[2 * LEVELS + 4 : 2 * LEVELS + 9]
    came = refs[2 * LEVELS + 9 : 2 * LEVELS + 14]
    staged, w_sem, p_sem, give_sem, get_sem, send_sem, recv_sem, out_sem = refs[2 * LEVELS + 14 :]

    gx = lax.axis_index("gx")
    gy = lax.axis_index("gy")
    x, z_high = gx // 2, gx % 2
    y, z_low, core = gy // 4, (gy // 2) % 2, gy % 2

    def flips(v):
        return (v, v + 1 - 2 * (v % 2), (v + 2) % 4, 3 - v)

    x_flips = flips(x)
    y_flips = flips(y)
    to_x = [(x_flips[j] * 2 + z_high, gy) for j in range(1, 4)]
    to_z_high = (gx + 1 - 2 * z_high, gy)
    to_y = [(gx, y_flips[j] * 4 + z_low * 2 + core) for j in range(1, 4)]
    to_z_low = (gx, gy + 2 - 4 * z_low)
    to_core = (gx, gy + 1 - 2 * core)
    level_devices = (
        [],
        [to_x[0]],
        [to_z_high],
        to_y,
        [to_y[0]],
        [to_z_low],
        [to_core],
    )
    level_picks = (
        (0,),
        (x % 2, 1 - x % 2),
        (z_high, 1 - z_high),
        y_flips,
        (y % 2, 1 - y % 2),
        (z_low, 1 - z_low),
        (core, 1 - core),
    )
    stage_devices = (to_x, [to_z_high], to_y, [to_z_low], [to_core])
    stage_picks = (x_flips, (z_high, 1 - z_high), y_flips, (z_low, 1 - z_low), (core, 1 - core))
    greeted = to_x + to_y + [to_z_high, to_z_low, to_core]

    barrier = pltpu.get_barrier_semaphore()
    for device in greeted:
        pl.semaphore_signal(barrier, inc=1, device_id=device, device_id_type=MESH)

    def weight_copy(unit):
        return pltpu.make_async_copy(w_ref.at[:, unit], w_buf.at[unit], w_sem.at[unit])

    def phase_part(level, pick, unit):
        return p_refs[level].at[level, pl.ds(pick * PICKED[level], PICKED[level]), unit]

    def phase_copy(level, unit):
        return pltpu.make_async_copy(
            phase_part(level, level_picks[level][0], unit),
            p_bufs[level].at[0, unit],
            p_sem.at[level, unit % LOCAL_SLOTS],
        )

    def phase_send(level, j, unit):
        lane = level + j - 1 + (2 if level > 3 else 0) - 1
        return pltpu.make_async_remote_copy(
            src_ref=phase_part(level, level_picks[level][j], unit),
            dst_ref=p_bufs[level].at[j, unit],
            send_sem=give_sem.at[lane, unit % STATIC_SLOTS],
            recv_sem=get_sem.at[lane, unit],
            device_id=level_devices[level][j - 1],
            device_id_type=MESH,
        )

    def held_part(stage, slot, j):
        pick = stage_picks[stage][j]
        if stage == 2:
            return held[stage].at[slot, :, pl.ds(pick * 4 * LOW, 4 * LOW)]
        if stage == 4:
            return held[stage].at[slot, :, pl.ds(pick * 8 * LOW, 8 * LOW)]
        return held[stage].at[slot, pick]

    def exchange(stage, j, chunk):
        slot = chunk % SLOTS
        lane = sum(PARTNERS[:stage]) + j - 1
        return pltpu.make_async_remote_copy(
            src_ref=held_part(stage, slot, j),
            dst_ref=came[stage].at[j - 1, chunk],
            send_sem=send_sem.at[lane, slot],
            recv_sem=recv_sem.at[lane, chunk],
            device_id=stage_devices[stage][j - 1],
            device_id_type=MESH,
        )

    def out_copy(chunk):
        return pltpu.make_async_copy(
            staged.at[chunk], out_ref.at[pl.ds(chunk * 2 * ROWS, 2 * ROWS)], out_sem.at[chunk]
        )

    def phase_rows(level, box, chunk, offset, count, stride):
        per = chunks_per_unit(level)
        flat = p_bufs[level].at[box, chunk // per].reshape(PICKED[level] * unit_rows(level), 128)
        start = (chunk % per) * (1 << low_bits(level)) + offset if per > 1 else offset
        return flat[pl.ds(start, count, stride=stride)]

    def keep(stage, slot, halves, start, real, imag):
        size = real.shape[0] // halves
        for half in range(halves):
            for part, value in enumerate((real, imag)):
                held[stage][slot, half, part, pl.ds(start, size)] = value[half * size : half * size + size]

    def own_and_came(stage, chunk):
        own = held_part(stage, chunk % SLOTS, 0)
        blocks = [own[0], own[1]]
        for j in range(PARTNERS[stage]):
            blocks += [came[stage][j, chunk, 0], came[stage][j, chunk, 1]]
        return blocks

    def first_stage(chunk):
        per = chunks_per_unit(0)
        slot = chunk % SLOTS
        flat = w_buf.at[chunk // per].reshape(128 * 16, 128)
        left = lax.broadcasted_iota(jnp.int32, (32, 128), 1) < 64
        for u in range(1 << low_bits(0)):
            row = (chunk % per) * (1 << low_bits(0)) + u
            for quarter in range(4):
                even = flat[pl.ds(quarter * 32 * 16 + 2 * row, 32, stride=16)]
                odd = flat[pl.ds(quarter * 32 * 16 + 2 * row + 1, 32, stride=16)]
                real = jnp.where(left, even, pltpu.roll(odd, 64, 1))
                imag = jnp.where(left, pltpu.roll(even, 64, 1), odd)
                angle = phase_rows(0, 0, chunk, quarter * 32 * 8 + u, 32, 8)
                real, imag = turned(real, imag, angle)
                held[0][slot, quarter, 0, pl.ds(u * 32, 32)] = real
                held[0][slot, quarter, 1, pl.ds(u * 32, 32)] = imag

    def pair_sum(out, size, rows, lanes, angles):
        total = None
        for box, angle in enumerate(angles):
            start = box * 2 * size + rows.start
            real = out[start : start + rows.stop - rows.start, lanes]
            imag = out[start + size : start + size + rows.stop - rows.start, lanes]
            value = turned(real, imag, angle)
            total = value if total is None else (total[0] + value[0], total[1] + value[1])
        return total

    def sides():
        return [(i, slice(i * 128, i * 128 + 128)) for i in range(2)]

    def second_stage(chunk):
        b = own_and_came(0, chunk)
        blocks = [b[0] + b[4], b[1] + b[5], b[2] + b[6], b[3] + b[7]]
        out = stacked_dot(blocks, mats_ref, 0)
        for u in range(LOW // 4):
            for i, lanes in sides():
                angles = [phase_rows(1, box, chunk, 2 * u + i, 32, unit_rows(1)) for box in range(2)]
                real, imag = pair_sum(out, HALF // 2, slice(u * 32, u * 32 + 32), lanes, angles)
                keep(1, chunk % SLOTS, 2, (2 * u + i) * 16, real, imag)

    def third_stage(chunk):
        out = stacked_dot(own_and_came(1, chunk), mats_ref, 0)
        for u in range(LOW // 2):
            for i, lanes in sides():
                angles = [phase_rows(2, box, chunk, 2 * u + i, 16, unit_rows(2)) for box in range(2)]
                sums = pair_sum(out, HALF // 2, slice(u * 16, u * 16 + 16), lanes, angles)
                for part in range(2):
                    held[2].at[chunk % SLOTS, part][pl.ds(2 * u + i, 16, stride=LOW)] = sums[part]

    def fourth_stage(chunk):
        size = 4 * LOW
        out = stacked_dot(own_and_came(2, chunk), mats_ref, 0)
        blocks = []
        for pair in range(2):
            parts = ([], [])
            for i, lanes in sides():
                total = None
                for box in (pair, pair + 2):
                    angle = phase_rows(3, box, chunk, i, size, 2)
                    start = box * 2 * size
                    value = turned(out[start : start + size, lanes], out[start + size : start + 2 * size, lanes], angle)
                    total = value if total is None else (total[0] + value[0], total[1] + value[1])
                parts[0].append(total[0])
                parts[1].append(total[1])
            blocks += [jnp.concatenate(p, axis=0) for p in parts]
        out = stacked_dot(blocks, mats_ref, 1)
        for i in range(2):
            for k, lanes in sides():
                angles = [phase_rows(4, box, chunk, 2 * i + k, size, 4) for box in range(2)]
                real, imag = pair_sum(out, 2 * size, slice(i * size, i * size + size), lanes, angles)
                keep(3, chunk % SLOTS, 2, (2 * i + k) * 2 * LOW, real, imag)

    def fifth_stage(chunk):
        size = 2 * LOW
        out = stacked_dot(own_and_came(3, chunk), mats_ref, 1)
        for low in range(4):
            for m, lanes in sides():
                angles = [phase_rows(5, box, chunk, 2 * low + m, size, 8) for box in range(2)]
                sums = pair_sum(out, 4 * size, slice(low * size, low * size + size), lanes, angles)
                for part in range(2):
                    held[4].at[chunk % SLOTS, part][pl.ds(2 * low + m, size, stride=8)] = sums[part]

    def last_stage(chunk):
        size = 8 * LOW
        out = stacked_dot(own_and_came(4, chunk), mats_ref, 1)
        rows = []
        for n, lanes in sides():
            angles = [phase_rows(6, box, chunk, n, size, 2) for box in range(2)]
            rows.append(jnp.concatenate(pair_sum(out, size, slice(0, size), lanes, angles), axis=1))
        high, low = split_value(jnp.concatenate(rows, axis=0))
        out = dot(high, last_ref[0]) + dot(low, last_ref[0]) + dot(high, last_ref[1])
        for n in range(2):
            for k in range(4):
                staged.at[chunk][pl.ds(n * 4 + k, size, stride=8)] = out[
                    n * size : n * size + size, k * 128 : k * 128 + 128
                ]

    stage_bodies = (first_stage, second_stage, third_stage, fourth_stage, fifth_stage, last_stage)

    def fetch(time):
        for level in range(LEVELS):
            ahead = time + AHEAD - OFFSETS[STAGE_OF[level]]
            per = chunks_per_unit(level)

            @pl.when((ahead >= 0) & (ahead < CHUNKS) & (ahead % per == 0))
            def _():
                phase_copy(level, ahead // per).start()
                if level == 0:
                    weight_copy(ahead // per).start()

    def give(time):
        for level in range(1, LEVELS):
            chunk = time - SEND_AT[level]
            per = chunks_per_unit(level)

            @pl.when((chunk >= 0) & (chunk < CHUNKS) & (chunk % per == 0))
            def _():
                unit = chunk // per

                @pl.when(unit >= STATIC_SLOTS)
                def _():
                    for j in range(1, BOXES[level]):
                        phase_send(level, j, unit - STATIC_SLOTS).wait_send()

                for j in range(1, BOXES[level]):
                    phase_send(level, j, unit).start()

    def work(time):
        for stage in range(STAGES):
            chunk = time - OFFSETS[stage]

            @pl.when((chunk >= 0) & (chunk < CHUNKS))
            def _():
                for level in range(LEVELS):
                    if STAGE_OF[level] == stage:
                        per = chunks_per_unit(level)

                        @pl.when(chunk % per == 0)
                        def _():
                            phase_copy(level, chunk // per).wait()
                            if level == 0:
                                weight_copy(chunk // per).wait()
                            for j in range(1, BOXES[level]):
                                phase_send(level, j, chunk // per).wait_recv()

                if stage > 0:
                    for j in range(1, PARTNERS[stage - 1] + 1):
                        exchange(stage - 1, j, chunk).wait_recv()
                if stage < STAGES - 1:

                    @pl.when(chunk >= SLOTS)
                    def _():
                        for j in range(1, PARTNERS[stage] + 1):
                            exchange(stage, j, chunk - SLOTS).wait_send()

                stage_bodies[stage](chunk)
                if stage < STAGES - 1:
                    for j in range(1, PARTNERS[stage] + 1):
                        exchange(stage, j, chunk).start()
                else:
                    out_copy(chunk).start()

    def early(time, carry):
        fetch(time)
        return carry

    lax.fori_loop(-AHEAD, 0, early, 0)
    pl.semaphore_wait(barrier, len(greeted))

    def lead(time, carry):
        give(time)
        return carry

    lax.fori_loop(min(SEND_AT), 0, lead, 0)

    def step(time, carry):
        fetch(time)
        give(time)
        work(time)
        return carry

    lax.fori_loop(0, CHUNKS + OFFSETS[-1], step, 0)

    def finish(chunk, carry):
        for stage in range(STAGES - 1):
            for j in range(1, PARTNERS[stage] + 1):
                exchange(stage, j, chunk).wait_send()
        return carry

    lax.fori_loop(CHUNKS - SLOTS, CHUNKS, finish, 0)
    for level in range(1, LEVELS):

        def given(unit, carry):
            for j in range(1, BOXES[level]):
                phase_send(level, j, unit).wait_send()
            return carry

        lax.fori_loop(units(level) - STATIC_SLOTS, units(level), given, 0)

    def drain(chunk, carry):
        out_copy(chunk).wait()
        return carry

    lax.fori_loop(0, CHUNKS, drain, 0)


def hand_on(in_ref, out_ref, held, in_sem, out_sem):
    size = out_ref.shape[0] // PIECES
    reads = []
    writes = []
    for k in range(PIECES):
        rows = pl.ds(k * size, size)
        reads.append(pltpu.make_async_copy(in_ref.at[rows], held.at[rows], in_sem.at[k]))
        writes.append(pltpu.make_async_copy(held.at[rows], out_ref.at[rows], out_sem.at[k]))
    for read in reads:
        read.start()
    for read, write in zip(reads, writes):
        read.wait()
        write.start()
    for write in writes:
        write.wait()


def shards(weights, phases):
    mats, last = refine_matrices()
    views = [
        phases.reshape(LEVELS, sel_count(level), units(level), unit_rows(level), 128)
        for level in range(LEVELS)
    ]
    anywhere = pl.BlockSpec(memory_space=pl.ANY)
    vmem = pl.BlockSpec(memory_space=pltpu.VMEM)

    def buffer(*shape):
        return pltpu.VMEM(shape + (128,), jnp.float32)

    scratch = [buffer(4, 128, 16)]
    scratch += [
        buffer(BOXES[level], units(level), PICKED[level], unit_rows(level)) for level in range(LEVELS)
    ]
    scratch += [
        buffer(SLOTS, 4, 2, HALF // 2),
        buffer(SLOTS, 2, 2, HALF // 2),
        buffer(SLOTS, 2, HALF),
        buffer(SLOTS, 2, 2, HALF // 2),
        buffer(SLOTS, 2, HALF),
    ]
    scratch += [
        buffer(3, CHUNKS, 2, HALF // 2),
        buffer(1, CHUNKS, 2, HALF // 2),
        buffer(3, CHUNKS, 2, HALF // 4),
        buffer(1, CHUNKS, 2, HALF // 2),
        buffer(1, CHUNKS, 2, HALF // 2),
    ]
    scratch += [
        buffer(CHUNKS, 2 * ROWS),
        pltpu.SemaphoreType.DMA((4,)),
        pltpu.SemaphoreType.DMA((LEVELS, LOCAL_SLOTS)),
        pltpu.SemaphoreType.DMA((8, STATIC_SLOTS)),
        pltpu.SemaphoreType.DMA((8, CHUNKS)),
        pltpu.SemaphoreType.DMA((9, SLOTS)),
        pltpu.SemaphoreType.DMA((9, CHUNKS)),
        pltpu.SemaphoreType.DMA((CHUNKS,)),
    ]
    result = pl.pallas_call(
        kernel,
        out_shape=jax.ShapeDtypeStruct(weights.shape, jnp.float32),
        in_specs=[anywhere] * (LEVELS + 1) + [vmem] * 2,
        out_specs=anywhere,
        scratch_shapes=scratch,
        compiler_params=pltpu.CompilerParams(
            collective_id=0, has_side_effects=True, vmem_limit_bytes=58 * 2**20
        ),
    )(weights.reshape(128, 4, 16, 128), *views, jnp.asarray(mats), jnp.asarray(last))
    return pl.pallas_call(
        hand_on,
        out_shape=jax.ShapeDtypeStruct(weights.shape, jnp.float32),
        in_specs=[anywhere],
        out_specs=anywhere,
        scratch_shapes=[
            buffer(*weights.shape[:1]),
            pltpu.SemaphoreType.DMA((PIECES,)),
            pltpu.SemaphoreType.DMA((PIECES,)),
        ],
    )(result)


def solution(mesh):
    return jax.shard_map(
        shards,
        mesh=mesh,
        in_specs=(P(("gx", "gy"), None), P(None, ("gx", "gy"), None)),
        out_specs=P(("gx", "gy"), None),
        check_vma=False,
    )
```

```python
import functools
import math

import jax
import jax.numpy as jnp
import numpy as np
from jax import lax
from jax.experimental import pallas as pl
from jax.experimental.pallas import tpu as pltpu
from jax.sharding import PartitionSpec as P

MESH = pl.DeviceIdType.MESH
LEVELS = 7
CHUNK_BITS = 3
CHUNKS = 1 << CHUNK_BITS
ROWS = 4096 // CHUNKS
HALF = ROWS // 2
LOW = 1 << (7 - CHUNK_BITS)
STAGES = 6
OFFSETS = (0, 2, 4, 6, 8, 10)
SLOTS = 4
AHEAD = 3
PIECES = 8
LOCAL_SLOTS = 4
STATIC_SLOTS = 4
BOXES = (1, 2, 2, 4, 2, 2, 2)
PICKED = (128, 32, 16, 4, 4, 2, 1)
STAGE_OF = (0, 1, 2, 3, 3, 4, 5)
SEND_AT = (0, 0, -1, 0, 0, -2, 0)
PARTNERS = (3, 1, 3, 1, 1)


def low_bits(level):
    return 5 - CHUNK_BITS + level


def unit_rows(level):
    return max(8, 1 << low_bits(level))


def units(level):
    return (1 << (5 + level)) // unit_rows(level)


def sel_count(level):
    return 1 << (7 - level)


def chunks_per_unit(level):
    return CHUNKS // units(level)


def series(func, degree):
    top = 3.140625**2
    nodes = (np.cos((np.arange(64) + 0.5) * np.pi / 64) + 1.0) * top / 2
    fit = np.polynomial.chebyshev.Chebyshev.fit(nodes, func(np.sqrt(nodes)), degree, domain=[0.0, top])
    return [float(np.float32(c)) for c in fit.convert(kind=np.polynomial.Polynomial).coef]


COS_COEF = series(np.cos, 6)
SIN_COEF = series(lambda r: np.sin(r) / r, 5)


def horner(coef, square):
    total = jnp.full_like(square, coef[-1])
    total = coef[-1] * square + coef[-2]
    for c in reversed(coef[:-2]):
        total = total * square + c
    return total


def cos_sin(angle):
    square = angle * angle
    return horner(COS_COEF, square), horner(SIN_COEF, square) * angle


def refine_matrices():
    nodes = np.cos((2.0 * np.arange(8) + 1.0) * math.pi / 16.0)
    sides = []
    for child in range(2):
        points = (nodes + 2.0 * child - 1.0) / 2.0
        lagrange = np.ones((8, 8))
        for j in range(8):
            for m in range(8):
                if m != j:
                    lagrange[j] *= (points - nodes[m]) / (nodes[j] - nodes[m])
        sides.append(lagrange)
    eye = np.eye(8)
    first = np.concatenate([np.kron(k, eye) for k in sides], axis=1)
    second = np.concatenate([np.kron(eye, k) for k in sides], axis=1)
    zero = np.zeros_like(first)

    def split(matrix):
        matrix = np.asarray(matrix, np.float32)
        high = matrix.astype(jnp.bfloat16)
        low = (matrix - high.astype(np.float32)).astype(jnp.bfloat16)
        return high, low

    mats = []
    for pair in (first, second):
        high, low = split(np.block([[pair, zero], [zero, pair]]))
        mats.append(np.stack([np.concatenate([high, high]), np.concatenate([low, low])]))
    last = np.zeros((256, 512))
    for slot in range(2):
        for child in range(2):
            edge = second[:, 64 * child : 64 * child + 64]
            col = 256 * slot + 128 * child
            last[64 * slot : 64 * slot + 64, col : col + 64] = edge
            last[128 + 64 * slot : 192 + 64 * slot, col + 64 : col + 128] = edge
    high, low = split(last)
    return np.stack(mats), np.stack([high, low])


def split_value(x):
    high = x.astype(jnp.bfloat16)
    low = (x - high.astype(jnp.float32)).astype(jnp.bfloat16)
    return high, low


def stacked_dot(blocks, mats, which):
    high, low = split_value(jnp.concatenate(blocks, axis=0))
    wide = jnp.concatenate([high, low], axis=1)
    return dot(wide, mats[which, 0]) + dot(wide, mats[which, 1])


def turned(real, imag, angle):
    cosine, sine = cos_sin(angle)
    return cosine * real - sine * imag, sine * real + cosine * imag


def dot(a, b):
    return jnp.dot(a, b, preferred_element_type=jnp.float32)


def kernel(w_ref, *refs):
    p_refs = refs[:LEVELS]
    mats_ref, last_ref, out_ref = refs[LEVELS : LEVELS + 3]
    w_buf = refs[LEVELS + 3]
    p_bufs = refs[LEVELS + 4 : 2 * LEVELS + 4]
    held = refs[2 * LEVELS + 4 : 2 * LEVELS + 9]
    came = refs[2 * LEVELS + 9 : 2 * LEVELS + 14]
    staged, w_sem, p_sem, give_sem, get_sem, send_sem, recv_sem, out_sem = refs[2 * LEVELS + 14 :]

    gx = lax.axis_index("gx")
    gy = lax.axis_index("gy")
    x, z_high = gx // 2, gx % 2
    y, z_low, core = gy // 4, (gy // 2) % 2, gy % 2

    def flips(v):
        return (v, v + 1 - 2 * (v % 2), (v + 2) % 4, 3 - v)

    x_flips = flips(x)
    y_flips = flips(y)
    to_x = [(x_flips[j] * 2 + z_high, gy) for j in range(1, 4)]
    to_z_high = (gx + 1 - 2 * z_high, gy)
    to_y = [(gx, y_flips[j] * 4 + z_low * 2 + core) for j in range(1, 4)]
    to_z_low = (gx, gy + 2 - 4 * z_low)
    to_core = (gx, gy + 1 - 2 * core)
    level_devices = (
        [],
        [to_x[0]],
        [to_z_high],
        to_y,
        [to_y[0]],
        [to_z_low],
        [to_core],
    )
    level_picks = (
        (0,),
        (x % 2, 1 - x % 2),
        (z_high, 1 - z_high),
        y_flips,
        (y % 2, 1 - y % 2),
        (z_low, 1 - z_low),
        (core, 1 - core),
    )
    stage_devices = (to_x, [to_z_high], to_y, [to_z_low], [to_core])
    stage_picks = (x_flips, (z_high, 1 - z_high), y_flips, (z_low, 1 - z_low), (core, 1 - core))
    greeted = to_x + to_y + [to_z_high, to_z_low, to_core]

    barrier = pltpu.get_barrier_semaphore()
    for device in greeted:
        pl.semaphore_signal(barrier, inc=1, device_id=device, device_id_type=MESH)

    def weight_copy(unit):
        return pltpu.make_async_copy(w_ref.at[:, unit], w_buf.at[unit], w_sem.at[unit])

    def phase_part(level, pick, unit):
        return p_refs[level].at[level, pl.ds(pick * PICKED[level], PICKED[level]), unit]

    def phase_copy(level, unit):
        return pltpu.make_async_copy(
            phase_part(level, level_picks[level][0], unit),
            p_bufs[level].at[0, unit],
            p_sem.at[level, unit % LOCAL_SLOTS],
        )

    def phase_send(level, j, unit):
        lane = level + j - 1 + (2 if level > 3 else 0) - 1
        return pltpu.make_async_remote_copy(
            src_ref=phase_part(level, level_picks[level][j], unit),
            dst_ref=p_bufs[level].at[j, unit],
            send_sem=give_sem.at[lane, unit % STATIC_SLOTS],
            recv_sem=get_sem.at[lane, unit],
            device_id=level_devices[level][j - 1],
            device_id_type=MESH,
        )

    def held_part(stage, slot, j):
        pick = stage_picks[stage][j]
        if stage == 2:
            return held[stage].at[slot, :, pl.ds(pick * 4 * LOW, 4 * LOW)]
        if stage == 4:
            return held[stage].at[slot, :, pl.ds(pick * 8 * LOW, 8 * LOW)]
        return held[stage].at[slot, pick]

    def exchange(stage, j, chunk):
        slot = chunk % SLOTS
        lane = sum(PARTNERS[:stage]) + j - 1
        return pltpu.make_async_remote_copy(
            src_ref=held_part(stage, slot, j),
            dst_ref=came[stage].at[j - 1, chunk],
            send_sem=send_sem.at[lane, slot],
            recv_sem=recv_sem.at[lane, chunk],
            device_id=stage_devices[stage][j - 1],
            device_id_type=MESH,
        )

    def out_copy(chunk):
        return pltpu.make_async_copy(
            staged.at[chunk], out_ref.at[pl.ds(chunk * 2 * ROWS, 2 * ROWS)], out_sem.at[chunk]
        )

    def phase_rows(level, box, chunk, offset, count, stride):
        per = chunks_per_unit(level)
        flat = p_bufs[level].at[box, chunk // per].reshape(PICKED[level] * unit_rows(level), 128)
        start = (chunk % per) * (1 << low_bits(level)) + offset if per > 1 else offset
        return flat[pl.ds(start, count, stride=stride)]

    def keep(stage, slot, halves, start, real, imag):
        size = real.shape[0] // halves
        for half in range(halves):
            for part, value in enumerate((real, imag)):
                held[stage][slot, half, part, pl.ds(start, size)] = value[half * size : half * size + size]

    def own_and_came(stage, chunk):
        own = held_part(stage, chunk % SLOTS, 0)
        blocks = [own[0], own[1]]
        for j in range(PARTNERS[stage]):
            blocks += [came[stage][j, chunk, 0], came[stage][j, chunk, 1]]
        return blocks

    def first_stage(chunk):
        per = chunks_per_unit(0)
        slot = chunk % SLOTS
        flat = w_buf.at[chunk // per].reshape(128 * 16, 128)
        left = lax.broadcasted_iota(jnp.int32, (32, 128), 1) < 64
        for u in range(1 << low_bits(0)):
            row = (chunk % per) * (1 << low_bits(0)) + u
            for quarter in range(4):
                even = flat[pl.ds(quarter * 32 * 16 + 2 * row, 32, stride=16)]
                odd = flat[pl.ds(quarter * 32 * 16 + 2 * row + 1, 32, stride=16)]
                real = jnp.where(left, even, pltpu.roll(odd, 64, 1))
                imag = jnp.where(left, pltpu.roll(even, 64, 1), odd)
                angle = phase_rows(0, 0, chunk, quarter * 32 * 8 + u, 32, 8)
                real, imag = turned(real, imag, angle)
                held[0][slot, quarter, 0, pl.ds(u * 32, 32)] = real
                held[0][slot, quarter, 1, pl.ds(u * 32, 32)] = imag

    def pair_sum(out, size, rows, lanes, angles):
        total = None
        for box, angle in enumerate(angles):
            start = box * 2 * size + rows.start
            real = out[start : start + rows.stop - rows.start, lanes]
            imag = out[start + size : start + size + rows.stop - rows.start, lanes]
            value = turned(real, imag, angle)
            total = value if total is None else (total[0] + value[0], total[1] + value[1])
        return total

    def sides():
        return [(i, slice(i * 128, i * 128 + 128)) for i in range(2)]

    def second_stage(chunk):
        b = own_and_came(0, chunk)
        blocks = [b[0] + b[4], b[1] + b[5], b[2] + b[6], b[3] + b[7]]
        out = stacked_dot(blocks, mats_ref, 0)
        for u in range(LOW // 4):
            for i, lanes in sides():
                angles = [phase_rows(1, box, chunk, 2 * u + i, 32, unit_rows(1)) for box in range(2)]
                real, imag = pair_sum(out, HALF // 2, slice(u * 32, u * 32 + 32), lanes, angles)
                keep(1, chunk % SLOTS, 2, (2 * u + i) * 16, real, imag)

    def third_stage(chunk):
        out = stacked_dot(own_and_came(1, chunk), mats_ref, 0)
        for u in range(LOW // 2):
            for i, lanes in sides():
                angles = [phase_rows(2, box, chunk, 2 * u + i, 16, unit_rows(2)) for box in range(2)]
                sums = pair_sum(out, HALF // 2, slice(u * 16, u * 16 + 16), lanes, angles)
                for part in range(2):
                    held[2].at[chunk % SLOTS, part][pl.ds(2 * u + i, 16, stride=LOW)] = sums[part]

    def fourth_stage(chunk):
        size = 4 * LOW
        out = stacked_dot(own_and_came(2, chunk), mats_ref, 0)
        blocks = []
        for pair in range(2):
            parts = ([], [])
            for i, lanes in sides():
                total = None
                for box in (pair, pair + 2):
                    angle = phase_rows(3, box, chunk, i, size, 2)
                    start = box * 2 * size
                    value = turned(out[start : start + size, lanes], out[start + size : start + 2 * size, lanes], angle)
                    total = value if total is None else (total[0] + value[0], total[1] + value[1])
                parts[0].append(total[0])
                parts[1].append(total[1])
            blocks += [jnp.concatenate(p, axis=0) for p in parts]
        out = stacked_dot(blocks, mats_ref, 1)
        for i in range(2):
            for k, lanes in sides():
                angles = [phase_rows(4, box, chunk, 2 * i + k, size, 4) for box in range(2)]
                real, imag = pair_sum(out, 2 * size, slice(i * size, i * size + size), lanes, angles)
                keep(3, chunk % SLOTS, 2, (2 * i + k) * 2 * LOW, real, imag)

    def fifth_stage(chunk):
        size = 2 * LOW
        out = stacked_dot(own_and_came(3, chunk), mats_ref, 1)
        for low in range(4):
            for m, lanes in sides():
                angles = [phase_rows(5, box, chunk, 2 * low + m, size, 8) for box in range(2)]
                sums = pair_sum(out, 4 * size, slice(low * size, low * size + size), lanes, angles)
                for part in range(2):
                    held[4].at[chunk % SLOTS, part][pl.ds(2 * low + m, size, stride=8)] = sums[part]

    def last_stage(chunk):
        size = 8 * LOW
        out = stacked_dot(own_and_came(4, chunk), mats_ref, 1)
        rows = []
        for n, lanes in sides():
            angles = [phase_rows(6, box, chunk, n, size, 2) for box in range(2)]
            rows.append(jnp.concatenate(pair_sum(out, size, slice(0, size), lanes, angles), axis=1))
        high, low = split_value(jnp.concatenate(rows, axis=0))
        out = dot(high, last_ref[0]) + dot(low, last_ref[0]) + dot(high, last_ref[1])
        for n in range(2):
            for k in range(4):
                staged.at[chunk][pl.ds(n * 4 + k, size, stride=8)] = out[
                    n * size : n * size + size, k * 128 : k * 128 + 128
                ]

    stage_bodies = (first_stage, second_stage, third_stage, fourth_stage, fifth_stage, last_stage)

    def fetch(time):
        for level in range(LEVELS):
            ahead = time + AHEAD - OFFSETS[STAGE_OF[level]]
            per = chunks_per_unit(level)

            @pl.when((ahead >= 0) & (ahead < CHUNKS) & (ahead % per == 0))
            def _():
                phase_copy(level, ahead // per).start()
                if level == 0:
                    weight_copy(ahead // per).start()

    def give(time):
        for level in range(1, LEVELS):
            chunk = time - SEND_AT[level]
            per = chunks_per_unit(level)

            @pl.when((chunk >= 0) & (chunk < CHUNKS) & (chunk % per == 0))
            def _():
                unit = chunk // per

                @pl.when(unit >= STATIC_SLOTS)
                def _():
                    for j in range(1, BOXES[level]):
                        phase_send(level, j, unit - STATIC_SLOTS).wait_send()

                for j in range(1, BOXES[level]):
                    phase_send(level, j, unit).start()

    def work(time):
        for stage in range(STAGES):
            chunk = time - OFFSETS[stage]

            @pl.when((chunk >= 0) & (chunk < CHUNKS))
            def _():
                for level in range(LEVELS):
                    if STAGE_OF[level] == stage:
                        per = chunks_per_unit(level)

                        @pl.when(chunk % per == 0)
                        def _():
                            phase_copy(level, chunk // per).wait()
                            if level == 0:
                                weight_copy(chunk // per).wait()
                            for j in range(1, BOXES[level]):
                                phase_send(level, j, chunk // per).wait_recv()

                if stage > 0:
                    for j in range(1, PARTNERS[stage - 1] + 1):
                        exchange(stage - 1, j, chunk).wait_recv()
                if stage < STAGES - 1:

                    @pl.when(chunk >= SLOTS)
                    def _():
                        for j in range(1, PARTNERS[stage] + 1):
                            exchange(stage, j, chunk - SLOTS).wait_send()

                stage_bodies[stage](chunk)
                if stage < STAGES - 1:
                    for j in range(1, PARTNERS[stage] + 1):
                        exchange(stage, j, chunk).start()
                else:
                    out_copy(chunk).start()

    def early(time, carry):
        fetch(time)
        return carry

    lax.fori_loop(-AHEAD, 0, early, 0)
    pl.semaphore_wait(barrier, len(greeted))

    def lead(time, carry):
        give(time)
        return carry

    lax.fori_loop(min(SEND_AT), 0, lead, 0)

    def step(time, carry):
        fetch(time)
        give(time)
        work(time)
        return carry

    lax.fori_loop(0, CHUNKS + OFFSETS[-1], step, 0)

    def finish(chunk, carry):
        for stage in range(STAGES - 1):
            for j in range(1, PARTNERS[stage] + 1):
                exchange(stage, j, chunk).wait_send()
        return carry

    lax.fori_loop(CHUNKS - SLOTS, CHUNKS, finish, 0)
    for level in range(1, LEVELS):

        def given(unit, carry):
            for j in range(1, BOXES[level]):
                phase_send(level, j, unit).wait_send()
            return carry

        lax.fori_loop(units(level) - STATIC_SLOTS, units(level), given, 0)

    def drain(chunk, carry):
        out_copy(chunk).wait()
        return carry

    lax.fori_loop(0, CHUNKS, drain, 0)


def hand_on(in_ref, out_ref, held, in_sem, out_sem):
    size = out_ref.shape[0] // PIECES
    reads = []
    writes = []
    for k in range(PIECES):
        rows = pl.ds(k * size, size)
        reads.append(pltpu.make_async_copy(in_ref.at[rows], held.at[rows], in_sem.at[k]))
        writes.append(pltpu.make_async_copy(held.at[rows], out_ref.at[rows], out_sem.at[k]))
    for read in reads:
        read.start()
    for read, write in zip(reads, writes):
        read.wait()
        write.start()
    for write in writes:
        write.wait()


def shards(weights, phases):
    mats, last = refine_matrices()
    views = [
        phases.reshape(LEVELS, sel_count(level), units(level), unit_rows(level), 128)
        for level in range(LEVELS)
    ]
    anywhere = pl.BlockSpec(memory_space=pl.ANY)
    vmem = pl.BlockSpec(memory_space=pltpu.VMEM)

    def buffer(*shape):
        return pltpu.VMEM(shape + (128,), jnp.float32)

    scratch = [buffer(4, 128, 16)]
    scratch += [
        buffer(BOXES[level], units(level), PICKED[level], unit_rows(level)) for level in range(LEVELS)
    ]
    scratch += [
        buffer(SLOTS, 4, 2, HALF // 2),
        buffer(SLOTS, 2, 2, HALF // 2),
        buffer(SLOTS, 2, HALF),
        buffer(SLOTS, 2, 2, HALF // 2),
        buffer(SLOTS, 2, HALF),
    ]
    scratch += [
        buffer(3, CHUNKS, 2, HALF // 2),
        buffer(1, CHUNKS, 2, HALF // 2),
        buffer(3, CHUNKS, 2, HALF // 4),
        buffer(1, CHUNKS, 2, HALF // 2),
        buffer(1, CHUNKS, 2, HALF // 2),
    ]
    scratch += [
        buffer(CHUNKS, 2 * ROWS),
        pltpu.SemaphoreType.DMA((4,)),
        pltpu.SemaphoreType.DMA((LEVELS, LOCAL_SLOTS)),
        pltpu.SemaphoreType.DMA((8, STATIC_SLOTS)),
        pltpu.SemaphoreType.DMA((8, CHUNKS)),
        pltpu.SemaphoreType.DMA((9, SLOTS)),
        pltpu.SemaphoreType.DMA((9, CHUNKS)),
        pltpu.SemaphoreType.DMA((CHUNKS,)),
    ]
    result = pl.pallas_call(
        kernel,
        out_shape=jax.ShapeDtypeStruct(weights.shape, jnp.float32),
        in_specs=[anywhere] * (LEVELS + 1) + [vmem] * 2,
        out_specs=anywhere,
        scratch_shapes=scratch,
        compiler_params=pltpu.CompilerParams(
            collective_id=0, has_side_effects=True, vmem_limit_bytes=58 * 2**20
        ),
    )(weights.reshape(128, 4, 16, 128), *views, jnp.asarray(mats), jnp.asarray(last))
    return pl.pallas_call(
        hand_on,
        out_shape=jax.ShapeDtypeStruct(weights.shape, jnp.float32),
        in_specs=[anywhere],
        out_specs=anywhere,
        scratch_shapes=[
            buffer(*weights.shape[:1]),
            pltpu.SemaphoreType.DMA((PIECES,)),
            pltpu.SemaphoreType.DMA((PIECES,)),
        ],
    )(result)


def solution(mesh):
    return jax.shard_map(
        shards,
        mesh=mesh,
        in_specs=(P(("gx", "gy"), None), P(None, ("gx", "gy"), None)),
        out_specs=P(("gx", "gy"), None),
        check_vma=False,
    )
```
